32 devices in a mesh: dp: 8 (over z, x), tensor: 4 (over y, core).
Axes of the slice: x: 2, y: 2, z: 4, core: 2. Of those that a mesh axis runs over, the one named last changes fastest.
Arguments:
- inputs: bfloat16 [256, 8192], P('dp'), may hold values from -6 to 6
- gate_weight: bfloat16 [8192, 28, 1024], P('dp', None, 'tensor'), may hold values from -0.0625 to 0.0625
- up_weight: bfloat16 [8192, 28, 1024], P('dp', None, 'tensor'), may hold values from -0.0625 to 0.0625
- down_weight: bfloat16 [28, 1024, 8192], P(None, 'tensor', 'dp'), may hold values from -0.03125 to 0.03125
Outputs:
- mixed: float32 [256, 8192], P('tensor', 'dp')
The draws below stay inside these ranges and needn't reach their ends.
All inputs are finite; a program needn't handle non-finite values.
Results may differ from the reference program's by a relative error of at most 0.0029.
Values may be sent and summed in bfloat16 or wider, within the bound.
A program may use at most 192 MiB of HBM per device.

```python
import math
import jax
import jax.numpy as jnp
import numpy as np
from jax import lax

D = 8192
HA = 28
HB = 1024
FF = 28672
ROWS = 256


def level_of(rng, extent, split, low, top_value):
    loudness, own = 1.0, jax.random.fold_in(rng, 6)
    for position, parts in split:
        draws = jnp.exp(jax.random.uniform(jax.random.fold_in(own, position), (parts,), jnp.float32, low / len(split), top_value / len(split)))
        loudness = loudness * jnp.repeat(draws, extent[position] // parts).reshape([-1 if axis == position else 1 for axis in range(len(extent))])
    return loudness


def gaussian(rng, extent, spread, most, split=(), kind=jnp.bfloat16):
    drawn = jax.random.normal(rng, extent, jnp.float32) * spread
    if len(split) > 0:
        drawn = level_of(rng, extent, split, -0.22, 0.18) * drawn
    return jnp.clip(drawn, min=-most, max=most).astype(kind)


def setup_inputs(seed: int = 0) -> dict:
    key_list = jax.random.split(jax.random.key(seed), 5)
    return {
        "inputs": gaussian(key_list[0], (ROWS, D), 1.0, 6.0, ((0, 8),)),
        "gate_weight": gaussian(key_list[1], (D, HA, HB), D ** -0.5, 0.0625, ((0, 8), (2, 4))),
        "up_weight": gaussian(key_list[2], (D, HA, HB), D ** -0.5, 0.0625, ((0, 8), (2, 4))),
        "down_weight": gaussian(key_list[3], (HA, HB, D), FF ** -0.5, 0.03125, ((1, 4), (2, 8))),
    }


def sylvester_table(order):
    index = np.arange(order)
    common = index[:, None] & index[None, :]
    parity = np.zeros((order, order), np.int64)
    for level in range(max(order.bit_length(), 1)):
        parity = parity ^ common >> level & 1
    return (1 - 2 * parity).astype(np.float32)

def paley_table():
    prime = 13
    residues = [base_value * base_value % prime for base_value in range(1, prime)]
    jacobsthal = np.zeros((prime, prime), np.float32)
    for row_index in range(prime):
        for col_index in range(prime):
            offset = (col_index - row_index) % prime
            if offset != 0:
                jacobsthal[row_index, col_index] = 1.0 if offset in residues else -1.0
    conference = np.zeros((prime + 1, prime + 1), np.float32)
    conference[0, 1:] = 1.0
    conference[1:, 0] = 1.0
    conference[1:, 1:] = jacobsthal
    upper_block = np.array([[1.0, 1.0], [1.0, -1.0]], np.float32)
    lower_block = np.array([[1.0, -1.0], [-1.0, -1.0]], np.float32)
    return (np.kron(conference, upper_block) + np.kron(np.eye(prime + 1, dtype=np.float32), lower_block)).astype(np.float32)

def reference(inputs, gate_weight, up_weight, down_weight):
    row_count = inputs.shape[0]
    hidden_width = HA * HB
    gate = jnp.dot(inputs, gate_weight.reshape(D, hidden_width), preferred_element_type=jnp.float32)
    upward = jnp.dot(inputs, up_weight.reshape(D, hidden_width), preferred_element_type=jnp.float32)
    hidden = (jax.nn.silu(gate) * upward).reshape(row_count, HA, HB)
    large_table = jnp.asarray(sylvester_table(HB)).astype(jnp.float32)
    small_table = jnp.asarray(paley_table()).astype(jnp.float32)
    turned = jnp.einsum('rab,bc->rac', hidden, large_table, precision=lax.Precision.HIGHEST)
    turned = jnp.einsum('rac,ad->rdc', turned, small_table, precision=lax.Precision.HIGHEST)
    rotated = (turned / math.sqrt(hidden_width)).astype(jnp.bfloat16).reshape(row_count, hidden_width)
    return jnp.dot(rotated, down_weight.reshape(hidden_width, D), preferred_element_type=jnp.float32)
```

```python
import functools
import math

import jax
import jax.numpy as jnp
import numpy as np
from jax import lax
from jax.experimental import pallas as pl
from jax.experimental.pallas import tpu as pltpu
from jax.sharding import PartitionSpec as P

RING = 4
LAG = 2


def sylvester_table(order):
    index = np.arange(order)
    common = index[:, None] & index[None, :]
    parity = np.zeros((order, order), np.int64)
    for level in range(max(order.bit_length(), 1)):
        parity = parity ^ common >> level & 1
    return (1 - 2 * parity).astype(np.float32)


def paley_table():
    prime = 13
    residues = [base_value * base_value % prime for base_value in range(1, prime)]
    jacobsthal = np.zeros((prime, prime), np.float32)
    for row_index in range(prime):
        for col_index in range(prime):
            offset = (col_index - row_index) % prime
            if offset != 0:
                jacobsthal[row_index, col_index] = 1.0 if offset in residues else -1.0
    conference = np.zeros((prime + 1, prime + 1), np.float32)
    conference[0, 1:] = 1.0
    conference[1:, 0] = 1.0
    conference[1:, 1:] = jacobsthal
    upper_block = np.array([[1.0, 1.0], [1.0, -1.0]], np.float32)
    lower_block = np.array([[1.0, -1.0], [-1.0, -1.0]], np.float32)
    return (
        np.kron(conference, upper_block) + np.kron(np.eye(prime + 1, dtype=np.float32), lower_block)
    ).astype(np.float32)


def encode(value):
    square = value * value
    return (value * jnp.abs(value) * square).astype(jnp.bfloat16)


def decode(code):
    wide = code.astype(jnp.float32)
    root = lax.rsqrt(lax.rsqrt(jnp.abs(wide)))
    return jnp.where(wide < 0, -root, root)


def partner_of(axis, bit):
    me = lax.axis_index(axis)
    high = lax.rem(me // (1 << bit), 2)
    return me + (1 - 2 * high) * (1 << bit), high


def hidden_kernel(halvings, doublings, factor, *refs):
    x_ref, gate_ref, up_ref, table_ref, out_ref = refs[:5]
    rest = list(refs[5:])
    weights, part, turned = rest[:3]
    del rest[:3]
    sends, rest = rest[: halvings + doublings], rest[halvings + doublings :]
    arrivals, rest = rest[: halvings + doublings], rest[halvings + doublings :]
    keeps, rest = rest[:halvings], rest[halvings:]
    weight_sem, send_sem, recv_sem = rest
    count, _, block = gate_ref.shape
    rows = x_ref.shape[0]
    places = [("dp", bit) + partner_of("dp", bit) for bit in range(halvings)]
    places += [("tensor", bit) + partner_of("tensor", bit) for bit in range(doublings)]

    def fetch(chunk, slot):
        return [
            pltpu.make_async_copy(source.at[chunk], weights.at[slot, which], weight_sem.at[slot, which])
            for which, source in enumerate((gate_ref, up_ref))
        ]

    def transfer(stage, chunk):
        axis, _, partner, _ = places[stage]
        return pltpu.make_async_remote_copy(
            src_ref=sends[stage].at[chunk],
            dst_ref=arrivals[stage].at[chunk],
            send_sem=send_sem.at[stage, chunk],
            recv_sem=recv_sem.at[stage, chunk],
            device_id={axis: partner},
            device_id_type=pl.DeviceIdType.MESH,
        )

    for copy in fetch(0, 0):
        copy.start()
    barrier = pltpu.get_barrier_semaphore()
    for axis, _, partner, _ in places:
        pl.semaphore_signal(barrier, inc=1, device_id={axis: partner}, device_id_type=pl.DeviceIdType.MESH)
    pl.semaphore_wait(barrier, len(places))

    def multiply(chunk):
        slot = lax.rem(chunk, 2)

        @pl.when(chunk + 1 < count)
        def _():
            for copy in fetch(chunk + 1, 1 - slot):
                copy.start()

        for copy in fetch(chunk, slot):
            copy.wait()
        for which in range(2):
            part[:, which * block : (which + 1) * block] = jnp.dot(
                x_ref[...], weights[slot, which], preferred_element_type=jnp.float32
            )
        half = rows // 2
        high = places[0][3]
        theirs = pl.multiple_of((1 - high) * half, half)
        ours = pl.multiple_of(high * half, half)
        sends[0][chunk] = encode(part[pl.ds(theirs, half), :])
        transfer(0, chunk).start()
        keeps[0][lax.rem(chunk, RING)] = part[pl.ds(ours, half), :]

    def halve(stage, chunk):
        transfer(stage - 1, chunk).wait_recv()
        slot = lax.rem(chunk, RING)
        half = rows >> (stage + 1)
        high = places[stage][3]
        theirs = pl.ds(pl.multiple_of((1 - high) * half, half), half)
        ours = pl.ds(pl.multiple_of(high * half, half), half)
        sends[stage][chunk] = encode(keeps[stage - 1][slot, theirs, :] + decode(arrivals[stage - 1][chunk, theirs, :]))
        transfer(stage, chunk).start()
        keeps[stage][slot] = keeps[stage - 1][slot, ours, :] + decode(arrivals[stage - 1][chunk, ours, :])

    def activate(chunk):
        transfer(halvings - 1, chunk).wait_recv()
        both = keeps[halvings - 1][lax.rem(chunk, RING)] + decode(arrivals[halvings - 1][chunk])
        gate, upward = both[:, :block], both[:, block:]
        hidden = gate / (1.0 + jnp.exp(-gate)) * upward
        own = hidden.shape[0]
        first = hidden.astype(jnp.bfloat16)
        left = hidden - first.astype(jnp.float32)
        second = left.astype(jnp.bfloat16)
        third = (left - second.astype(jnp.float32)).astype(jnp.bfloat16)
        pieces = jnp.dot(
            jnp.concatenate((first, second, third), axis=0), table_ref[...], preferred_element_type=jnp.float32
        )
        store(halvings, chunk, pieces[:own] + pieces[own : 2 * own] + pieces[2 * own :])

    def store(stage, chunk, value):
        if stage == halvings + doublings:
            turned[chunk] = value
        else:
            sends[stage][chunk] = value
            transfer(stage, chunk).start()

    def butterfly(stage, chunk):
        transfer(stage, chunk).wait_recv()
        sign = (1 - 2 * places[stage][3]).astype(jnp.float32)
        store(stage + 1, chunk, sign * sends[stage][chunk] + arrivals[stage][chunk])

    steps = [multiply]
    steps += [functools.partial(halve, stage) for stage in range(1, halvings)]
    steps += [activate]
    steps += [functools.partial(butterfly, halvings + level) for level in range(doublings)]

    def iteration(turn, carry):
        for order, step in enumerate(steps):
            chunk = turn - order * LAG

            @pl.when((chunk >= 0) & (chunk < count))
            def _(step=step, chunk=chunk):
                step(chunk)

        return carry

    lax.fori_loop(0, count + (len(steps) - 1) * LAG, iteration, 0)

    paley = paley_table()
    scale = 1.0 / math.sqrt(factor)
    band = 16

    def mix(index, carry):
        place = pl.ds(pl.multiple_of(index * band, band), band)
        for lane in range(0, block, 128):
            values = [turned[a, place, lane : lane + 128] for a in range(count)]
            for b in range(count):
                total = values[0] if paley[0, b] > 0 else -values[0]
                for a in range(1, count):
                    total = total + values[a] if paley[a, b] > 0 else total - values[a]
                out_ref[place, b * block + lane : b * block + lane + 128] = (total * scale).astype(jnp.bfloat16)
        return carry

    lax.fori_loop(0, turned.shape[1] // band, mix, 0)

    def drain(chunk, carry):
        for stage in range(halvings + doublings):
            transfer(stage, chunk).wait_send()
        return carry

    lax.fori_loop(0, count, drain, 0)


def rotated_hidden(columns, gate_weight, up_weight, groups, tensor):
    depth, count, block = gate_weight.shape
    rows = columns.shape[0]
    halvings = groups.bit_length() - 1
    doublings = tensor.bit_length() - 1
    own = rows // groups
    shape = (2,) * halvings + (own, depth)
    order = tuple(range(halvings))[::-1] + (halvings, halvings + 1)
    columns = columns.reshape(shape).transpose(order).reshape(rows, depth)
    table = jnp.asarray(sylvester_table(block), jnp.bfloat16)
    halves = [pltpu.VMEM((count, rows >> (level + 1), 2 * block), jnp.bfloat16) for level in range(halvings)]
    wholes = [pltpu.VMEM((count, own, block), jnp.float32) for _ in range(doublings)]
    keeps = [pltpu.VMEM((RING, rows >> (level + 1), 2 * block), jnp.float32) for level in range(halvings)]
    stages = halvings + doublings
    vmem = pl.BlockSpec(memory_space=pltpu.VMEM)
    hbm = pl.BlockSpec(memory_space=pl.ANY)
    return pl.pallas_call(
        functools.partial(hidden_kernel, halvings, doublings, count * block * tensor),
        out_shape=jax.ShapeDtypeStruct((own, count * block), jnp.bfloat16),
        in_specs=[vmem, hbm, hbm, vmem],
        out_specs=vmem,
        scratch_shapes=[
            pltpu.VMEM((2, 2, depth, block), jnp.bfloat16),
            pltpu.VMEM((rows, 2 * block), jnp.float32),
            pltpu.VMEM((count, own, block), jnp.float32),
            *halves,
            *wholes,
            *halves,
            *wholes,
            *keeps,
            pltpu.SemaphoreType.DMA((2, 2)),
            pltpu.SemaphoreType.DMA((stages, count)),
            pltpu.SemaphoreType.DMA((stages, count)),
        ],
        compiler_params=pltpu.CompilerParams(collective_id=0, has_side_effects=True, vmem_limit_bytes=56 * 2**20),
        cost_estimate=pl.CostEstimate(
            flops=4 * rows * depth * count * block,
            bytes_accessed=4 * depth * count * block,
            transcendentals=4 * rows * count * block,
        ),
    )(columns, jnp.transpose(gate_weight, (1, 0, 2)), jnp.transpose(up_weight, (1, 0, 2)), table)


def per_device(groups, tensor, inputs, gate_weight, up_weight, down_weight):
    kernel_a, block_e, width = down_weight.shape
    columns = lax.all_to_all(inputs, "dp", split_axis=1, concat_axis=0, tiled=True)
    rotated = rotated_hidden(columns, gate_weight, up_weight, groups, tensor)
    piece = lax.all_gather(rotated, "dp", axis=0, tiled=True)
    partial_sums = jnp.dot(
        piece, down_weight.reshape(kernel_a * block_e, width), preferred_element_type=jnp.float32
    )
    return lax.psum_scatter(partial_sums, "tensor", scatter_dimension=0, tiled=True)


def solution(mesh):
    return jax.shard_map(
        functools.partial(per_device, mesh.shape["dp"], mesh.shape["tensor"]),
        mesh=mesh,
        in_specs=(
            P("dp", None),
            P("dp", None, "tensor"),
            P("dp", None, "tensor"),
            P(None, "tensor", "dp"),
        ),
        out_specs=P("tensor", "dp"),
        check_vma=False,
    )
```

```python
import functools
import math

import jax
import jax.numpy as jnp
import numpy as np
from jax import lax
from jax.experimental import pallas as pl
from jax.experimental.pallas import tpu as pltpu
from jax.sharding import PartitionSpec as P

RING = 4
LAG = 2


def sylvester_table(order):
    index = np.arange(order)
    common = index[:, None] & index[None, :]
    parity = np.zeros((order, order), np.int64)
    for level in range(max(order.bit_length(), 1)):
        parity = parity ^ common >> level & 1
    return (1 - 2 * parity).astype(np.float32)


def paley_table():
    prime = 13
    residues = [base_value * base_value % prime for base_value in range(1, prime)]
    jacobsthal = np.zeros((prime, prime), np.float32)
    for row_index in range(prime):
        for col_index in range(prime):
            offset = (col_index - row_index) % prime
            if offset != 0:
                jacobsthal[row_index, col_index] = 1.0 if offset in residues else -1.0
    conference = np.zeros((prime + 1, prime + 1), np.float32)
    conference[0, 1:] = 1.0
    conference[1:, 0] = 1.0
    conference[1:, 1:] = jacobsthal
    upper_block = np.array([[1.0, 1.0], [1.0, -1.0]], np.float32)
    lower_block = np.array([[1.0, -1.0], [-1.0, -1.0]], np.float32)
    return (
        np.kron(conference, upper_block) + np.kron(np.eye(prime + 1, dtype=np.float32), lower_block)
    ).astype(np.float32)


def encode(value):
    square = value * value
    return (value * jnp.abs(value) * square).astype(jnp.bfloat16)


def decode(code):
    wide = code.astype(jnp.float32)
    root = lax.rsqrt(lax.rsqrt(jnp.abs(wide)))
    return jnp.where(wide < 0, -root, root)


def partner_of(axis, bit):
    me = lax.axis_index(axis)
    high = lax.rem(me // (1 << bit), 2)
    return me + (1 - 2 * high) * (1 << bit), high


def hidden_kernel(halvings, doublings, factor, *refs):
    x_ref, gate_ref, up_ref, table_ref, out_ref = refs[:5]
    rest = list(refs[5:])
    weights, part, turned = rest[:3]
    del rest[:3]
    sends, rest = rest[: halvings + doublings], rest[halvings + doublings :]
    arrivals, rest = rest[: halvings + doublings], rest[halvings + doublings :]
    keeps, rest = rest[:halvings], rest[halvings:]
    weight_sem, send_sem, recv_sem = rest
    count, _, block = gate_ref.shape
    rows = x_ref.shape[0]
    places = [("dp", bit) + partner_of("dp", bit) for bit in range(halvings)]
    places += [("tensor", bit) + partner_of("tensor", bit) for bit in range(doublings)]

    def fetch(chunk, slot):
        return [
            pltpu.make_async_copy(source.at[chunk], weights.at[slot, which], weight_sem.at[slot, which])
            for which, source in enumerate((gate_ref, up_ref))
        ]

    def transfer(stage, chunk):
        axis, _, partner, _ = places[stage]
        return pltpu.make_async_remote_copy(
            src_ref=sends[stage].at[chunk],
            dst_ref=arrivals[stage].at[chunk],
            send_sem=send_sem.at[stage, chunk],
            recv_sem=recv_sem.at[stage, chunk],
            device_id={axis: partner},
            device_id_type=pl.DeviceIdType.MESH,
        )

    for copy in fetch(0, 0):
        copy.start()
    barrier = pltpu.get_barrier_semaphore()
    for axis, _, partner, _ in places:
        pl.semaphore_signal(barrier, inc=1, device_id={axis: partner}, device_id_type=pl.DeviceIdType.MESH)
    pl.semaphore_wait(barrier, len(places))

    def multiply(chunk):
        slot = lax.rem(chunk, 2)

        @pl.when(chunk + 1 < count)
        def _():
            for copy in fetch(chunk + 1, 1 - slot):
                copy.start()

        for copy in fetch(chunk, slot):
            copy.wait()
        for which in range(2):
            part[:, which * block : (which + 1) * block] = jnp.dot(
                x_ref[...], weights[slot, which], preferred_element_type=jnp.float32
            )
        half = rows // 2
        high = places[0][3]
        theirs = pl.multiple_of((1 - high) * half, half)
        ours = pl.multiple_of(high * half, half)
        sends[0][chunk] = encode(part[pl.ds(theirs, half), :])
        transfer(0, chunk).start()
        keeps[0][lax.rem(chunk, RING)] = part[pl.ds(ours, half), :]

    def halve(stage, chunk):
        transfer(stage - 1, chunk).wait_recv()
        slot = lax.rem(chunk, RING)
        half = rows >> (stage + 1)
        high = places[stage][3]
        theirs = pl.ds(pl.multiple_of((1 - high) * half, half), half)
        ours = pl.ds(pl.multiple_of(high * half, half), half)
        sends[stage][chunk] = encode(keeps[stage - 1][slot, theirs, :] + decode(arrivals[stage - 1][chunk, theirs, :]))
        transfer(stage, chunk).start()
        keeps[stage][slot] = keeps[stage - 1][slot, ours, :] + decode(arrivals[stage - 1][chunk, ours, :])

    def activate(chunk):
        transfer(halvings - 1, chunk).wait_recv()
        both = keeps[halvings - 1][lax.rem(chunk, RING)] + decode(arrivals[halvings - 1][chunk])
        gate, upward = both[:, :block], both[:, block:]
        hidden = gate / (1.0 + jnp.exp(-gate)) * upward
        own = hidden.shape[0]
        first = hidden.astype(jnp.bfloat16)
        left = hidden - first.astype(jnp.float32)
        second = left.astype(jnp.bfloat16)
        third = (left - second.astype(jnp.float32)).astype(jnp.bfloat16)
        pieces = jnp.dot(
            jnp.concatenate((first, second, third), axis=0), table_ref[...], preferred_element_type=jnp.float32
        )
        store(halvings, chunk, pieces[:own] + pieces[own : 2 * own] + pieces[2 * own :])

    def store(stage, chunk, value):
        if stage == halvings + doublings:
            turned[chunk] = value
        else:
            sends[stage][chunk] = value
            transfer(stage, chunk).start()

    def butterfly(stage, chunk):
        transfer(stage, chunk).wait_recv()
        sign = (1 - 2 * places[stage][3]).astype(jnp.float32)
        store(stage + 1, chunk, sign * sends[stage][chunk] + arrivals[stage][chunk])

    steps = [multiply]
    steps += [functools.partial(halve, stage) for stage in range(1, halvings)]
    steps += [activate]
    steps += [functools.partial(butterfly, halvings + level) for level in range(doublings)]

    def iteration(turn, carry):
        for order, step in enumerate(steps):
            chunk = turn - order * LAG

            @pl.when((chunk >= 0) & (chunk < count))
            def _(step=step, chunk=chunk):
                step(chunk)

        return carry

    lax.fori_loop(0, count + (len(steps) - 1) * LAG, iteration, 0)

    paley = paley_table()
    scale = 1.0 / math.sqrt(factor)
    band = 16

    def mix(index, carry):
        place = pl.ds(pl.multiple_of(index * band, band), band)
        for lane in range(0, block, 128):
            values = [turned[a, place, lane : lane + 128] for a in range(count)]
            for b in range(count):
                total = values[0] if paley[0, b] > 0 else -values[0]
                for a in range(1, count):
                    total = total + values[a] if paley[a, b] > 0 else total - values[a]
                out_ref[place, b * block + lane : b * block + lane + 128] = (total * scale).astype(jnp.bfloat16)
        return carry

    lax.fori_loop(0, turned.shape[1] // band, mix, 0)

    def drain(chunk, carry):
        for stage in range(halvings + doublings):
            transfer(stage, chunk).wait_send()
        return carry

    lax.fori_loop(0, count, drain, 0)


def rotated_hidden(columns, gate_weight, up_weight, groups, tensor):
    depth, count, block = gate_weight.shape
    rows = columns.shape[0]
    halvings = groups.bit_length() - 1
    doublings = tensor.bit_length() - 1
    own = rows // groups
    shape = (2,) * halvings + (own, depth)
    order = tuple(range(halvings))[::-1] + (halvings, halvings + 1)
    columns = columns.reshape(shape).transpose(order).reshape(rows, depth)
    table = jnp.asarray(sylvester_table(block), jnp.bfloat16)
    halves = [pltpu.VMEM((count, rows >> (level + 1), 2 * block), jnp.bfloat16) for level in range(halvings)]
    wholes = [pltpu.VMEM((count, own, block), jnp.float32) for _ in range(doublings)]
    keeps = [pltpu.VMEM((RING, rows >> (level + 1), 2 * block), jnp.float32) for level in range(halvings)]
    stages = halvings + doublings
    vmem = pl.BlockSpec(memory_space=pltpu.VMEM)
    hbm = pl.BlockSpec(memory_space=pl.ANY)
    return pl.pallas_call(
        functools.partial(hidden_kernel, halvings, doublings, count * block * tensor),
        out_shape=jax.ShapeDtypeStruct((own, count * block), jnp.bfloat16),
        in_specs=[vmem, hbm, hbm, vmem],
        out_specs=vmem,
        scratch_shapes=[
            pltpu.VMEM((2, 2, depth, block), jnp.bfloat16),
            pltpu.VMEM((rows, 2 * block), jnp.float32),
            pltpu.VMEM((count, own, block), jnp.float32),
            *halves,
            *wholes,
            *halves,
            *wholes,
            *keeps,
            pltpu.SemaphoreType.DMA((2, 2)),
            pltpu.SemaphoreType.DMA((stages, count)),
            pltpu.SemaphoreType.DMA((stages, count)),
        ],
        compiler_params=pltpu.CompilerParams(collective_id=0, has_side_effects=True, vmem_limit_bytes=56 * 2**20),
        cost_estimate=pl.CostEstimate(
            flops=4 * rows * depth * count * block,
            bytes_accessed=4 * depth * count * block,
            transcendentals=4 * rows * count * block,
        ),
    )(columns, jnp.transpose(gate_weight, (1, 0, 2)), jnp.transpose(up_weight, (1, 0, 2)), table)


def reversed_bits(axis, bits):
    me = lax.axis_index(axis)
    return sum(lax.rem(me // (1 << bit), 2) * (1 << (bits - 1 - bit)) for bit in range(bits))


def down_kernel(levels, folds, span, *refs):
    rotated_ref, down_ref, out_ref, gathered, weights, total = refs[:6]
    rest = list(refs[6:])
    sends, rest = rest[:folds], rest[folds:]
    arrivals, rest = rest[:folds], rest[folds:]
    keeps, rest = rest[:folds], rest[folds:]
    weight_sem, send_sem, recv_sem, fold_send_sem, fold_recv_sem = rest
    own = rotated_ref.shape[0]
    rows, width = total.shape
    chunks = gathered.shape[0]
    groups = 1 << levels
    block = out_ref.shape[0]
    tiles = max(1, min(4, width // 128))
    tile_width = width // tiles
    place = reversed_bits("dp", levels)
    spread = [partner_of("dp", levels - 1 - stage) for stage in range(levels)]
    folded = [partner_of("tensor", level) for level in range(folds)]

    def fetch(chunk):
        source = down_ref.at[pl.ds(pl.multiple_of(chunk * span, span), span), :]
        return pltpu.make_async_copy(source, weights.at[chunk], weight_sem.at[chunk])

    def prefetch(chunk, carry):
        fetch(chunk).start()
        return carry

    lax.fori_loop(0, chunks, prefetch, 0)
    barrier = pltpu.get_barrier_semaphore()
    for partner, _ in spread:
        pl.semaphore_signal(barrier, inc=1, device_id={"dp": partner}, device_id_type=pl.DeviceIdType.MESH)
    for partner, _ in folded:
        pl.semaphore_signal(barrier, inc=1, device_id={"tensor": partner}, device_id_type=pl.DeviceIdType.MESH)
    mine = pl.ds(pl.multiple_of(place * own, own), own)
    for chunk in range(chunks):
        gathered[chunk, mine, :] = rotated_ref[:, chunk * span : (chunk + 1) * span]
    pl.semaphore_wait(barrier, levels + folds)

    def transfer(stage, chunk):
        size = own << stage
        start = place // (1 << stage) * size
        held = gathered.at[chunk, pl.ds(pl.multiple_of(start, size), size), :]
        return pltpu.make_async_remote_copy(
            src_ref=held,
            dst_ref=held,
            send_sem=send_sem.at[stage, chunk],
            recv_sem=recv_sem.at[stage, chunk],
            device_id={"dp": spread[stage][0]},
            device_id_type=pl.DeviceIdType.MESH,
        )

    def relay(stage, chunk):
        if stage > 0:
            transfer(stage - 1, chunk).wait_recv()
        transfer(stage, chunk).start()

    def natural(block_index):
        return sum((block_index >> bit & 1) << (levels - 1 - bit) for bit in range(levels))

    def multiply(chunk):
        transfer(levels - 1, chunk).wait_recv()
        fetch(chunk).wait()
        left = jnp.concatenate(
            [gathered[chunk, natural(p) * own : (natural(p) + 1) * own, :] for p in range(groups)], axis=0
        )
        for tile in range(tiles):
            cols = slice(tile * tile_width, (tile + 1) * tile_width)
            total[:, cols] += jnp.dot(left, weights[chunk, :, cols], preferred_element_type=jnp.float32)

    total[...] = jnp.zeros_like(total)
    steps = [functools.partial(relay, stage) for stage in range(levels)] + [multiply]

    def iteration(turn, carry):
        for order, step in enumerate(steps):
            chunk = turn - order * LAG

            @pl.when((chunk >= 0) & (chunk < chunks))
            def _(step=step, chunk=chunk):
                step(chunk)

        return carry

    lax.fori_loop(0, chunks + (len(steps) - 1) * LAG, iteration, 0)

    def fold(level, tile):
        cols = pl.ds(tile * tile_width, tile_width)
        return pltpu.make_async_remote_copy(
            src_ref=sends[level].at[:, cols],
            dst_ref=arrivals[level].at[:, cols],
            send_sem=fold_send_sem.at[level, tile],
            recv_sem=fold_recv_sem.at[level, tile],
            device_id={"tensor": folded[level][0]},
            device_id_type=pl.DeviceIdType.MESH,
        )

    def part_of(level, index, bit):
        source = total if level == 0 else keeps[level - 1]
        return source, pl.ds(pl.multiple_of((2 * index + bit) * block, block), block)

    def give(level, tile):
        cols = slice(tile * tile_width, (tile + 1) * tile_width)
        for index in range(1 << (folds - 1 - level)):
            source, at = part_of(level, index, 1 - folded[level][1])
            sends[level][index * block : (index + 1) * block, cols] = source[at, cols]
        fold(level, tile).start()

    for tile in range(tiles):
        give(0, tile)
    for level in range(folds):
        for tile in range(tiles):
            cols = slice(tile * tile_width, (tile + 1) * tile_width)
            fold(level, tile).wait_recv()
            target = out_ref if level + 1 == folds else keeps[level]
            for index in range(1 << (folds - 1 - level)):
                source, at = part_of(level, index, folded[level][1])
                span_of = slice(index * block, (index + 1) * block)
                target[span_of, cols] = source[at, cols] + arrivals[level][span_of, cols]
            if level + 1 < folds:
                give(level + 1, tile)

    def drain(chunk, carry):
        for stage in range(levels):
            transfer(stage, chunk).wait_send()
        return carry

    lax.fori_loop(0, chunks, drain, 0)
    for level in range(folds):
        for tile in range(tiles):
            fold(level, tile).wait_send()


def mixed_rows(rotated, down_flat, count, groups, tensor):
    own, hidden = rotated.shape
    width = down_flat.shape[1]
    rows = own * groups
    levels = groups.bit_length() - 1
    folds = tensor.bit_length() - 1
    chunks = count // 2
    span = hidden // chunks
    block = rows // tensor
    tiles = max(1, min(4, width // 128))
    halves = [pltpu.VMEM((rows >> (level + 1), width), jnp.float32) for level in range(folds)]
    vmem = pl.BlockSpec(memory_space=pltpu.VMEM)
    return pl.pallas_call(
        functools.partial(down_kernel, levels, folds, span),
        out_shape=jax.ShapeDtypeStruct((block, width), jnp.float32),
        in_specs=[vmem, pl.BlockSpec(memory_space=pl.ANY)],
        out_specs=vmem,
        scratch_shapes=[
            pltpu.VMEM((chunks, rows, span), jnp.bfloat16),
            pltpu.VMEM((chunks, span, width), jnp.bfloat16),
            pltpu.VMEM((rows, width), jnp.float32),
            *halves,
            *halves,
            *halves,
            pltpu.SemaphoreType.DMA((chunks,)),
            pltpu.SemaphoreType.DMA((levels, chunks)),
            pltpu.SemaphoreType.DMA((levels, chunks)),
            pltpu.SemaphoreType.DMA((folds, tiles)),
            pltpu.SemaphoreType.DMA((folds, tiles)),
        ],
        compiler_params=pltpu.CompilerParams(collective_id=1, has_side_effects=True, vmem_limit_bytes=56 * 2**20),
        cost_estimate=pl.CostEstimate(
            flops=2 * rows * hidden * width, bytes_accessed=2 * hidden * width, transcendentals=0
        ),
    )(rotated, down_flat)


def per_device(groups, tensor, inputs, gate_weight, up_weight, down_weight):
    kernel_a, block_e, width = down_weight.shape
    columns = lax.all_to_all(inputs, "dp", split_axis=1, concat_axis=0, tiled=True)
    rotated = rotated_hidden(columns, gate_weight, up_weight, groups, tensor)
    return mixed_rows(rotated, down_weight.reshape(kernel_a * block_e, width), kernel_a, groups, tensor)


def solution(mesh):
    return jax.shard_map(
        functools.partial(per_device, mesh.shape["dp"], mesh.shape["tensor"]),
        mesh=mesh,
        in_specs=(
            P("dp", None),
            P("dp", None, "tensor"),
            P("dp", None, "tensor"),
            P(None, "tensor", "dp"),
        ),
        out_specs=P("tensor", "dp"),
        check_vma=False,
    )
```

```python
import functools
import math

import jax
import jax.numpy as jnp
import numpy as np
from jax import lax
from jax.experimental import pallas as pl
from jax.experimental.pallas import tpu as pltpu
from jax.sharding import PartitionSpec as P

RING = 4
LAG = 2


def sylvester_table(order):
    index = np.arange(order)
    common = index[:, None] & index[None, :]
    parity = np.zeros((order, order), np.int64)
    for level in range(max(order.bit_length(), 1)):
        parity = parity ^ common >> level & 1
    return (1 - 2 * parity).astype(np.float32)


def paley_table():
    prime = 13
    residues = [base_value * base_value % prime for base_value in range(1, prime)]
    jacobsthal = np.zeros((prime, prime), np.float32)
    for row_index in range(prime):
        for col_index in range(prime):
            offset = (col_index - row_index) % prime
            if offset != 0:
                jacobsthal[row_index, col_index] = 1.0 if offset in residues else -1.0
    conference = np.zeros((prime + 1, prime + 1), np.float32)
    conference[0, 1:] = 1.0
    conference[1:, 0] = 1.0
    conference[1:, 1:] = jacobsthal
    upper_block = np.array([[1.0, 1.0], [1.0, -1.0]], np.float32)
    lower_block = np.array([[1.0, -1.0], [-1.0, -1.0]], np.float32)
    return (
        np.kron(conference, upper_block) + np.kron(np.eye(prime + 1, dtype=np.float32), lower_block)
    ).astype(np.float32)


def encode(value):
    square = value * value
    return (value * jnp.abs(value) * square).astype(jnp.bfloat16)


def decode(code):
    wide = code.astype(jnp.float32)
    root = lax.rsqrt(lax.rsqrt(jnp.abs(wide)))
    return jnp.where(wide < 0, -root, root)


def partner_of(axis, bit):
    me = lax.axis_index(axis)
    high = lax.rem(me // (1 << bit), 2)
    return me + (1 - 2 * high) * (1 << bit), high


def bit_orders(bits, kinds):
    plain = tuple(range(bits))
    turned = plain[1:] + plain[:1]
    return [plain, turned][:kinds]


def choose(kind, values):
    first, second = values
    return first + kind * (second - first)


def place_of(index, order):
    top = len(order) - 1
    return sum((index // (1 << bit)) % 2 * (1 << (top - stage)) for stage, bit in enumerate(order))


def hidden_kernel(halvings, doublings, factor, *refs):
    x_ref, gate_ref, up_ref, table_ref, out_ref = refs[:5]
    rest = list(refs[5:])
    columns, weights, part, turned = rest[:4]
    del rest[:4]
    sends, rest = rest[: halvings + doublings], rest[halvings + doublings :]
    arrivals, rest = rest[: halvings + doublings], rest[halvings + doublings :]
    keeps, rest = rest[:halvings], rest[halvings:]
    weight_sem, send_sem, recv_sem, own_sem, spread_send_sem, spread_recv_sem = rest
    count, depth, block = gate_ref.shape
    own = x_ref.shape[0]
    groups = 1 << halvings
    rows = own * groups
    me = lax.axis_index("dp")
    orders = bit_orders(halvings, 2)
    tensor_places = [partner_of("tensor", bit) for bit in range(doublings)]
    by_bit = [partner_of("dp", bit) for bit in range(halvings)]

    def kind_of(chunk):
        return lax.rem(chunk, 6) // 5

    def toward(stage, chunk):
        if stage >= halvings:
            return "tensor", *tensor_places[stage - halvings]
        partner, high = (
            choose(kind_of(chunk), [by_bit[order[stage]][item] for order in orders]) for item in range(2)
        )
        return "dp", partner, high

    def fetch(chunk, slot):
        return [
            pltpu.make_async_copy(source.at[chunk], weights.at[slot, which], weight_sem.at[slot, which])
            for which, source in enumerate((gate_ref, up_ref))
        ]

    def transfer(stage, chunk):
        axis, partner, _ = toward(stage, chunk)
        return pltpu.make_async_remote_copy(
            src_ref=sends[stage].at[chunk],
            dst_ref=arrivals[stage].at[chunk],
            send_sem=send_sem.at[stage, chunk],
            recv_sem=recv_sem.at[stage, chunk],
            device_id={axis: partner},
            device_id_type=pl.DeviceIdType.MESH,
        )

    for copy in fetch(0, 0):
        copy.start()
    barrier = pltpu.get_barrier_semaphore()
    peers = [lax.rem(me + step, groups) for step in range(1, groups)]
    for peer in peers:
        pl.semaphore_signal(barrier, inc=1, device_id={"dp": peer}, device_id_type=pl.DeviceIdType.MESH)
    for partner, _ in tensor_places:
        pl.semaphore_signal(barrier, inc=1, device_id={"tensor": partner}, device_id_type=pl.DeviceIdType.MESH)
    mine = columns.at[0, pl.ds(pl.multiple_of(place_of(me, orders[0]) * own, own), own), :]

    def cut(target):
        return x_ref.at[:, pl.ds(pl.multiple_of(target * depth, depth), depth)]

    kept = pltpu.make_async_copy(cut(me), mine, own_sem)
    kept.start()
    pl.semaphore_wait(barrier, len(peers) + doublings)
    shares = [
        pltpu.make_async_remote_copy(
            src_ref=cut(peer),
            dst_ref=mine,
            send_sem=spread_send_sem.at[step],
            recv_sem=spread_recv_sem.at[step],
            device_id={"dp": peer},
            device_id_type=pl.DeviceIdType.MESH,
        )
        for step, peer in enumerate(peers)
    ]
    for share in shares:
        share.start()
    kept.wait()
    for share in shares:
        share.wait_recv()
    for index in range(groups):
        source, target = (place_of(index, order) * own for order in orders)
        columns[1, target : target + own, :] = columns[0, source : source + own, :]

    def multiply(chunk):
        slot = lax.rem(chunk, 2)

        @pl.when(chunk + 1 < count)
        def _():
            for copy in fetch(chunk + 1, 1 - slot):
                copy.start()

        for copy in fetch(chunk, slot):
            copy.wait()
        for which in range(2):
            part[:, which * block : (which + 1) * block] = jnp.dot(
                columns[kind_of(chunk)], weights[slot, which], preferred_element_type=jnp.float32
            )
        half = rows // 2
        high = toward(0, chunk)[2]
        theirs = pl.multiple_of((1 - high) * half, half)
        ours = pl.multiple_of(high * half, half)
        sends[0][chunk] = encode(part[pl.ds(theirs, half), :])
        transfer(0, chunk).start()
        keeps[0][lax.rem(chunk, RING)] = part[pl.ds(ours, half), :]

    def halve(stage, chunk):
        transfer(stage - 1, chunk).wait_recv()
        slot = lax.rem(chunk, RING)
        half = rows >> (stage + 1)
        high = toward(stage, chunk)[2]
        theirs = pl.ds(pl.multiple_of((1 - high) * half, half), half)
        ours = pl.ds(pl.multiple_of(high * half, half), half)
        sends[stage][chunk] = encode(keeps[stage - 1][slot, theirs, :] + decode(arrivals[stage - 1][chunk, theirs, :]))
        transfer(stage, chunk).start()
        keeps[stage][slot] = keeps[stage - 1][slot, ours, :] + decode(arrivals[stage - 1][chunk, ours, :])

    def activate(chunk):
        transfer(halvings - 1, chunk).wait_recv()
        both = keeps[halvings - 1][lax.rem(chunk, RING)] + decode(arrivals[halvings - 1][chunk])
        gate, upward = both[:, :block], both[:, block:]
        hidden = gate / (1.0 + jnp.exp(-gate)) * upward
        first = hidden.astype(jnp.bfloat16)
        left = hidden - first.astype(jnp.float32)
        second = left.astype(jnp.bfloat16)
        third = (left - second.astype(jnp.float32)).astype(jnp.bfloat16)
        pieces = jnp.dot(
            jnp.concatenate((first, second, third), axis=0), table_ref[...], preferred_element_type=jnp.float32
        )
        store(halvings, chunk, pieces[:own] + pieces[own : 2 * own] + pieces[2 * own :])

    def store(stage, chunk, value):
        if stage == halvings + doublings:
            turned[chunk] = value
        else:
            sends[stage][chunk] = value
            transfer(stage, chunk).start()

    def butterfly(stage, chunk):
        transfer(stage, chunk).wait_recv()
        sign = (1 - 2 * toward(stage, chunk)[2]).astype(jnp.float32)
        store(stage + 1, chunk, sign * sends[stage][chunk] + arrivals[stage][chunk])

    steps = [multiply]
    steps += [functools.partial(halve, stage) for stage in range(1, halvings)]
    steps += [activate]
    steps += [functools.partial(butterfly, halvings + level) for level in range(doublings)]

    def iteration(turn, carry):
        for order, step in enumerate(steps):
            chunk = turn - order * LAG

            @pl.when((chunk >= 0) & (chunk < count))
            def _(step=step, chunk=chunk):
                step(chunk)

        return carry

    lax.fori_loop(0, count + (len(steps) - 1) * LAG, iteration, 0)

    paley = paley_table()
    scale = 1.0 / math.sqrt(factor)
    band = 16

    def mix(index, carry):
        place = pl.ds(pl.multiple_of(index * band, band), band)
        for lane in range(0, block, 128):
            values = [turned[a, place, lane : lane + 128] for a in range(count)]
            for b in range(count):
                total = values[0] if paley[0, b] > 0 else -values[0]
                for a in range(1, count):
                    total = total + values[a] if paley[a, b] > 0 else total - values[a]
                out_ref[place, b * block + lane : b * block + lane + 128] = (total * scale).astype(jnp.bfloat16)
        return carry

    lax.fori_loop(0, turned.shape[1] // band, mix, 0)

    def drain(chunk, carry):
        for stage in range(halvings + doublings):
            transfer(stage, chunk).wait_send()
        return carry

    lax.fori_loop(0, count, drain, 0)
    for share in shares:
        share.wait_send()


def rotated_hidden(inputs, gate_weight, up_weight, groups, tensor):
    depth, count, block = gate_weight.shape
    own = inputs.shape[0]
    rows = own * groups
    halvings = groups.bit_length() - 1
    doublings = tensor.bit_length() - 1
    table = jnp.asarray(sylvester_table(block), jnp.bfloat16)
    halves = [pltpu.VMEM((count, rows >> (level + 1), 2 * block), jnp.bfloat16) for level in range(halvings)]
    wholes = [pltpu.VMEM((count, own, block), jnp.float32) for _ in range(doublings)]
    keeps = [pltpu.VMEM((RING, rows >> (level + 1), 2 * block), jnp.float32) for level in range(halvings)]
    stages = halvings + doublings
    vmem = pl.BlockSpec(memory_space=pltpu.VMEM)
    hbm = pl.BlockSpec(memory_space=pl.ANY)
    return pl.pallas_call(
        functools.partial(hidden_kernel, halvings, doublings, count * block * tensor),
        out_shape=jax.ShapeDtypeStruct((own, count * block), jnp.bfloat16),
        in_specs=[vmem, hbm, hbm, vmem],
        out_specs=vmem,
        scratch_shapes=[
            pltpu.VMEM((2, rows, depth), jnp.bfloat16),
            pltpu.VMEM((2, 2, depth, block), jnp.bfloat16),
            pltpu.VMEM((rows, 2 * block), jnp.float32),
            pltpu.VMEM((count, own, block), jnp.float32),
            *halves,
            *wholes,
            *halves,
            *wholes,
            *keeps,
            pltpu.SemaphoreType.DMA((2, 2)),
            pltpu.SemaphoreType.DMA((stages, count)),
            pltpu.SemaphoreType.DMA((stages, count)),
            pltpu.SemaphoreType.DMA,
            pltpu.SemaphoreType.DMA((groups - 1,)),
            pltpu.SemaphoreType.DMA((groups - 1,)),
        ],
        compiler_params=pltpu.CompilerParams(collective_id=0, has_side_effects=True, vmem_limit_bytes=56 * 2**20),
        cost_estimate=pl.CostEstimate(
            flops=4 * rows * depth * count * block,
            bytes_accessed=4 * depth * count * block,
            transcendentals=4 * rows * count * block,
        ),
    )(inputs, jnp.transpose(gate_weight, (1, 0, 2)), jnp.transpose(up_weight, (1, 0, 2)), table)


def reversed_bits(axis, bits):
    me = lax.axis_index(axis)
    return sum(lax.rem(me // (1 << bit), 2) * (1 << (bits - 1 - bit)) for bit in range(bits))


def down_kernel(levels, folds, span, *refs):
    rotated_ref, down_ref, out_ref, gathered, weights, total = refs[:6]
    rest = list(refs[6:])
    sends, rest = rest[:folds], rest[folds:]
    arrivals, rest = rest[:folds], rest[folds:]
    keeps, rest = rest[:folds], rest[folds:]
    weight_sem, send_sem, recv_sem, fold_send_sem, fold_recv_sem = rest
    own = rotated_ref.shape[0]
    rows, width = total.shape
    chunks = gathered.shape[0]
    groups = 1 << levels
    block = out_ref.shape[0]
    tiles = max(1, min(4, width // 128))
    tile_width = width // tiles
    place = reversed_bits("dp", levels)
    spread = [partner_of("dp", levels - 1 - stage) for stage in range(levels)]
    folded = [partner_of("tensor", level) for level in range(folds)]

    def fetch(chunk):
        source = down_ref.at[pl.ds(pl.multiple_of(chunk * span, span), span), :]
        return pltpu.make_async_copy(source, weights.at[chunk], weight_sem.at[chunk])

    def prefetch(chunk, carry):
        fetch(chunk).start()
        return carry

    lax.fori_loop(0, chunks, prefetch, 0)
    barrier = pltpu.get_barrier_semaphore()
    for partner, _ in spread:
        pl.semaphore_signal(barrier, inc=1, device_id={"dp": partner}, device_id_type=pl.DeviceIdType.MESH)
    for partner, _ in folded:
        pl.semaphore_signal(barrier, inc=1, device_id={"tensor": partner}, device_id_type=pl.DeviceIdType.MESH)
    mine = pl.ds(pl.multiple_of(place * own, own), own)
    for chunk in range(chunks):
        gathered[chunk, mine, :] = rotated_ref[:, chunk * span : (chunk + 1) * span]
    pl.semaphore_wait(barrier, levels + folds)

    def transfer(stage, chunk):
        size = own << stage
        start = place // (1 << stage) * size
        held = gathered.at[chunk, pl.ds(pl.multiple_of(start, size), size), :]
        return pltpu.make_async_remote_copy(
            src_ref=held,
            dst_ref=held,
            send_sem=send_sem.at[stage, chunk],
            recv_sem=recv_sem.at[stage, chunk],
            device_id={"dp": spread[stage][0]},
            device_id_type=pl.DeviceIdType.MESH,
        )

    def relay(stage, chunk):
        if stage > 0:
            transfer(stage - 1, chunk).wait_recv()
        transfer(stage, chunk).start()

    def natural(block_index):
        return sum((block_index >> bit & 1) << (levels - 1 - bit) for bit in range(levels))

    def multiply(chunk):
        transfer(levels - 1, chunk).wait_recv()
        fetch(chunk).wait()
        left = jnp.concatenate(
            [gathered[chunk, natural(p) * own : (natural(p) + 1) * own, :] for p in range(groups)], axis=0
        )
        for tile in range(tiles):
            cols = slice(tile * tile_width, (tile + 1) * tile_width)
            total[:, cols] += jnp.dot(left, weights[chunk, :, cols], preferred_element_type=jnp.float32)

    total[...] = jnp.zeros_like(total)
    steps = [functools.partial(relay, stage) for stage in range(levels)] + [multiply]

    def iteration(turn, carry):
        for order, step in enumerate(steps):
            chunk = turn - order * LAG

            @pl.when((chunk >= 0) & (chunk < chunks))
            def _(step=step, chunk=chunk):
                step(chunk)

        return carry

    lax.fori_loop(0, chunks + (len(steps) - 1) * LAG, iteration, 0)

    def fold(level, tile):
        cols = pl.ds(tile * tile_width, tile_width)
        return pltpu.make_async_remote_copy(
            src_ref=sends[level].at[:, cols],
            dst_ref=arrivals[level].at[:, cols],
            send_sem=fold_send_sem.at[level, tile],
            recv_sem=fold_recv_sem.at[level, tile],
            device_id={"tensor": folded[level][0]},
            device_id_type=pl.DeviceIdType.MESH,
        )

    def part_of(level, index, bit):
        source = total if level == 0 else keeps[level - 1]
        return source, pl.ds(pl.multiple_of((2 * index + bit) * block, block), block)

    def give(level, tile):
        cols = slice(tile * tile_width, (tile + 1) * tile_width)
        for index in range(1 << (folds - 1 - level)):
            source, at = part_of(level, index, 1 - folded[level][1])
            sends[level][index * block : (index + 1) * block, cols] = source[at, cols]
        fold(level, tile).start()

    for tile in range(tiles):
        give(0, tile)
    for level in range(folds):
        for tile in range(tiles):
            cols = slice(tile * tile_width, (tile + 1) * tile_width)
            fold(level, tile).wait_recv()
            target = out_ref if level + 1 == folds else keeps[level]
            for index in range(1 << (folds - 1 - level)):
                source, at = part_of(level, index, folded[level][1])
                span_of = slice(index * block, (index + 1) * block)
                target[span_of, cols] = source[at, cols] + arrivals[level][span_of, cols]
            if level + 1 < folds:
                give(level + 1, tile)

    def drain(chunk, carry):
        for stage in range(levels):
            transfer(stage, chunk).wait_send()
        return carry

    lax.fori_loop(0, chunks, drain, 0)
    for level in range(folds):
        for tile in range(tiles):
            fold(level, tile).wait_send()


def mixed_rows(rotated, down_flat, count, groups, tensor):
    own, hidden = rotated.shape
    width = down_flat.shape[1]
    rows = own * groups
    levels = groups.bit_length() - 1
    folds = tensor.bit_length() - 1
    chunks = count // 2
    span = hidden // chunks
    block = rows // tensor
    tiles = max(1, min(4, width // 128))
    halves = [pltpu.VMEM((rows >> (level + 1), width), jnp.float32) for level in range(folds)]
    vmem = pl.BlockSpec(memory_space=pltpu.VMEM)
    return pl.pallas_call(
        functools.partial(down_kernel, levels, folds, span),
        out_shape=jax.ShapeDtypeStruct((block, width), jnp.float32),
        in_specs=[vmem, pl.BlockSpec(memory_space=pl.ANY)],
        out_specs=vmem,
        scratch_shapes=[
            pltpu.VMEM((chunks, rows, span), jnp.bfloat16),
            pltpu.VMEM((chunks, span, width), jnp.bfloat16),
            pltpu.VMEM((rows, width), jnp.float32),
            *halves,
            *halves,
            *halves,
            pltpu.SemaphoreType.DMA((chunks,)),
            pltpu.SemaphoreType.DMA((levels, chunks)),
            pltpu.SemaphoreType.DMA((levels, chunks)),
            pltpu.SemaphoreType.DMA((folds, tiles)),
            pltpu.SemaphoreType.DMA((folds, tiles)),
        ],
        compiler_params=pltpu.CompilerParams(collective_id=1, has_side_effects=True, vmem_limit_bytes=56 * 2**20),
        cost_estimate=pl.CostEstimate(
            flops=2 * rows * hidden * width, bytes_accessed=2 * hidden * width, transcendentals=0
        ),
    )(rotated, down_flat)


def per_device(groups, tensor, inputs, gate_weight, up_weight, down_weight):
    kernel_a, block_e, width = down_weight.shape
    rotated = rotated_hidden(inputs, gate_weight, up_weight, groups, tensor)
    return mixed_rows(rotated, down_weight.reshape(kernel_a * block_e, width), kernel_a, groups, tensor)


def solution(mesh):
    return jax.shard_map(
        functools.partial(per_device, mesh.shape["dp"], mesh.shape["tensor"]),
        mesh=mesh,
        in_specs=(
            P("dp", None),
            P("dp", None, "tensor"),
            P("dp", None, "tensor"),
            P(None, "tensor", "dp"),
        ),
        out_specs=P("tensor", "dp"),
        check_vma=False,
    )
```

```python
import functools
import math

import jax
import jax.numpy as jnp
import numpy as np
from jax import lax
from jax.experimental import pallas as pl
from jax.experimental.pallas import tpu as pltpu
from jax.sharding import PartitionSpec as P

RING = 4
LAG = 3


def sylvester_table(order):
    index = np.arange(order)
    common = index[:, None] & index[None, :]
    parity = np.zeros((order, order), np.int64)
    for level in range(max(order.bit_length(), 1)):
        parity = parity ^ common >> level & 1
    return (1 - 2 * parity).astype(np.float32)


def paley_table():
    prime = 13
    residues = [base_value * base_value % prime for base_value in range(1, prime)]
    jacobsthal = np.zeros((prime, prime), np.float32)
    for row_index in range(prime):
        for col_index in range(prime):
            offset = (col_index - row_index) % prime
            if offset != 0:
                jacobsthal[row_index, col_index] = 1.0 if offset in residues else -1.0
    conference = np.zeros((prime + 1, prime + 1), np.float32)
    conference[0, 1:] = 1.0
    conference[1:, 0] = 1.0
    conference[1:, 1:] = jacobsthal
    upper_block = np.array([[1.0, 1.0], [1.0, -1.0]], np.float32)
    lower_block = np.array([[1.0, -1.0], [-1.0, -1.0]], np.float32)
    return (
        np.kron(conference, upper_block) + np.kron(np.eye(prime + 1, dtype=np.float32), lower_block)
    ).astype(np.float32)


def encode(value):
    square = value * value
    return (value * jnp.abs(value) * square).astype(jnp.bfloat16)


def decode(code):
    wide = code.astype(jnp.float32)
    root = lax.rsqrt(lax.rsqrt(jnp.abs(wide)))
    return jnp.where(wide < 0, -root, root)


def partner_of(axis, bit):
    me = lax.axis_index(axis)
    high = lax.rem(me // (1 << bit), 2)
    return me + (1 - 2 * high) * (1 << bit), high


def bit_orders(bits, kinds):
    plain = tuple(range(bits))
    turned = plain[1:] + plain[:1]
    return [plain, turned][:kinds]


def choose(kind, values):
    first, second = values
    return first + kind * (second - first)


def place_of(index, order):
    top = len(order) - 1
    return sum((index // (1 << bit)) % 2 * (1 << (top - stage)) for stage, bit in enumerate(order))


def hidden_kernel(halvings, doublings, factor, *refs):
    x_ref, gate_ref, up_ref, table_ref, out_ref = refs[:5]
    rest = list(refs[5:])
    columns, weights, part, turned = rest[:4]
    del rest[:4]
    sends, rest = rest[: halvings + doublings], rest[halvings + doublings :]
    arrivals, rest = rest[: halvings + doublings], rest[halvings + doublings :]
    keeps, rest = rest[:halvings], rest[halvings:]
    weight_sem, send_sem, recv_sem, own_sem, spread_send_sem, spread_recv_sem = rest
    count, depth, block = gate_ref.shape
    own = x_ref.shape[0]
    groups = 1 << halvings
    rows = own * groups
    me = lax.axis_index("dp")
    orders = bit_orders(halvings, 2)
    tensor_places = [partner_of("tensor", bit) for bit in range(doublings)]
    by_bit = [partner_of("dp", bit) for bit in range(halvings)]

    def kind_of(chunk):
        return lax.rem(chunk, 6) // 5

    def toward(stage, chunk):
        if stage >= halvings:
            return "tensor", *tensor_places[stage - halvings]
        partner, high = (
            choose(kind_of(chunk), [by_bit[order[stage]][item] for order in orders]) for item in range(2)
        )
        return "dp", partner, high

    def fetch(chunk, slot):
        return [
            pltpu.make_async_copy(source.at[chunk], weights.at[slot, which], weight_sem.at[slot, which])
            for which, source in enumerate((gate_ref, up_ref))
        ]

    def transfer(stage, chunk):
        axis, partner, _ = toward(stage, chunk)
        return pltpu.make_async_remote_copy(
            src_ref=sends[stage].at[chunk],
            dst_ref=arrivals[stage].at[chunk],
            send_sem=send_sem.at[stage, chunk],
            recv_sem=recv_sem.at[stage, chunk],
            device_id={axis: partner},
            device_id_type=pl.DeviceIdType.MESH,
        )

    for copy in fetch(0, 0):
        copy.start()
    barrier = pltpu.get_barrier_semaphore()
    peers = [lax.rem(me + step, groups) for step in range(1, groups)]
    for peer in peers:
        pl.semaphore_signal(barrier, inc=1, device_id={"dp": peer}, device_id_type=pl.DeviceIdType.MESH)
    for partner, _ in tensor_places:
        pl.semaphore_signal(barrier, inc=1, device_id={"tensor": partner}, device_id_type=pl.DeviceIdType.MESH)
    mine = columns.at[0, pl.ds(pl.multiple_of(place_of(me, orders[0]) * own, own), own), :]

    def cut(target):
        return x_ref.at[:, pl.ds(pl.multiple_of(target * depth, depth), depth)]

    kept = pltpu.make_async_copy(cut(me), mine, own_sem)
    kept.start()
    pl.semaphore_wait(barrier, len(peers) + doublings)
    shares = [
        pltpu.make_async_remote_copy(
            src_ref=cut(peer),
            dst_ref=mine,
            send_sem=spread_send_sem.at[step],
            recv_sem=spread_recv_sem.at[step],
            device_id={"dp": peer},
            device_id_type=pl.DeviceIdType.MESH,
        )
        for step, peer in enumerate(peers)
    ]
    for share in shares:
        share.start()
    kept.wait()
    for share in shares:
        share.wait_recv()
    for index in range(groups):
        source, target = (place_of(index, order) * own for order in orders)
        columns[1, target : target + own, :] = columns[0, source : source + own, :]

    def multiply(chunk):
        slot = lax.rem(chunk, 2)

        @pl.when(chunk + 1 < count)
        def _():
            for copy in fetch(chunk + 1, 1 - slot):
                copy.start()

        for copy in fetch(chunk, slot):
            copy.wait()
        for which in range(2):
            part[:, which * block : (which + 1) * block] = jnp.dot(
                columns[kind_of(chunk)], weights[slot, which], preferred_element_type=jnp.float32
            )
        half = rows // 2
        high = toward(0, chunk)[2]
        theirs = pl.multiple_of((1 - high) * half, half)
        ours = pl.multiple_of(high * half, half)
        sends[0][chunk] = encode(part[pl.ds(theirs, half), :])
        transfer(0, chunk).start()
        keeps[0][lax.rem(chunk, RING)] = part[pl.ds(ours, half), :]

    def halve(stage, chunk):
        transfer(stage - 1, chunk).wait_recv()
        slot = lax.rem(chunk, RING)
        half = rows >> (stage + 1)
        high = toward(stage, chunk)[2]
        theirs = pl.ds(pl.multiple_of((1 - high) * half, half), half)
        ours = pl.ds(pl.multiple_of(high * half, half), half)
        sends[stage][chunk] = encode(keeps[stage - 1][slot, theirs, :] + decode(arrivals[stage - 1][chunk, theirs, :]))
        transfer(stage, chunk).start()
        keeps[stage][slot] = keeps[stage - 1][slot, ours, :] + decode(arrivals[stage - 1][chunk, ours, :])

    def activate(chunk):
        transfer(halvings - 1, chunk).wait_recv()
        both = keeps[halvings - 1][lax.rem(chunk, RING)] + decode(arrivals[halvings - 1][chunk])
        gate, upward = both[:, :block], both[:, block:]
        hidden = gate / (1.0 + jnp.exp(-gate)) * upward
        first = hidden.astype(jnp.bfloat16)
        left = hidden - first.astype(jnp.float32)
        second = left.astype(jnp.bfloat16)
        third = (left - second.astype(jnp.float32)).astype(jnp.bfloat16)
        pieces = jnp.dot(
            jnp.concatenate((first, second, third), axis=0), table_ref[...], preferred_element_type=jnp.float32
        )
        store(halvings, chunk, pieces[:own] + pieces[own : 2 * own] + pieces[2 * own :])

    def store(stage, chunk, value):
        if stage == halvings + doublings:
            turned[chunk] = value
        else:
            sends[stage][chunk] = value
            transfer(stage, chunk).start()

    def butterfly(stage, chunk):
        transfer(stage, chunk).wait_recv()
        sign = (1 - 2 * toward(stage, chunk)[2]).astype(jnp.float32)
        store(stage + 1, chunk, sign * sends[stage][chunk] + arrivals[stage][chunk])

    steps = [multiply]
    steps += [functools.partial(halve, stage) for stage in range(1, halvings)]
    steps += [activate]
    steps += [functools.partial(butterfly, halvings + level) for level in range(doublings)]

    def iteration(turn, carry):
        for order, step in enumerate(steps):
            chunk = turn - order * LAG

            @pl.when((chunk >= 0) & (chunk < count))
            def _(step=step, chunk=chunk):
                step(chunk)

        return carry

    lax.fori_loop(0, count + (len(steps) - 1) * LAG, iteration, 0)

    paley = paley_table()
    scale = 1.0 / math.sqrt(factor)
    band = 16

    def mix(index, carry):
        place = pl.ds(pl.multiple_of(index * band, band), band)
        for lane in range(0, block, 128):
            values = [turned[a, place, lane : lane + 128] for a in range(count)]
            for b in range(count):
                total = values[0] if paley[0, b] > 0 else -values[0]
                for a in range(1, count):
                    total = total + values[a] if paley[a, b] > 0 else total - values[a]
                out_ref[place, b * block + lane : b * block + lane + 128] = (total * scale).astype(jnp.bfloat16)
        return carry

    lax.fori_loop(0, turned.shape[1] // band, mix, 0)

    def drain(chunk, carry):
        for stage in range(halvings + doublings):
            transfer(stage, chunk).wait_send()
        return carry

    lax.fori_loop(0, count, drain, 0)
    for share in shares:
        share.wait_send()


def rotated_hidden(inputs, gate_weight, up_weight, groups, tensor):
    depth, count, block = gate_weight.shape
    own = inputs.shape[0]
    rows = own * groups
    halvings = groups.bit_length() - 1
    doublings = tensor.bit_length() - 1
    table = jnp.asarray(sylvester_table(block), jnp.bfloat16)
    halves = [pltpu.VMEM((count, rows >> (level + 1), 2 * block), jnp.bfloat16) for level in range(halvings)]
    wholes = [pltpu.VMEM((count, own, block), jnp.float32) for _ in range(doublings)]
    keeps = [pltpu.VMEM((RING, rows >> (level + 1), 2 * block), jnp.float32) for level in range(halvings)]
    stages = halvings + doublings
    vmem = pl.BlockSpec(memory_space=pltpu.VMEM)
    hbm = pl.BlockSpec(memory_space=pl.ANY)
    return pl.pallas_call(
        functools.partial(hidden_kernel, halvings, doublings, count * block * tensor),
        out_shape=jax.ShapeDtypeStruct((own, count * block), jnp.bfloat16),
        in_specs=[vmem, hbm, hbm, vmem],
        out_specs=vmem,
        scratch_shapes=[
            pltpu.VMEM((2, rows, depth), jnp.bfloat16),
            pltpu.VMEM((2, 2, depth, block), jnp.bfloat16),
            pltpu.VMEM((rows, 2 * block), jnp.float32),
            pltpu.VMEM((count, own, block), jnp.float32),
            *halves,
            *wholes,
            *halves,
            *wholes,
            *keeps,
            pltpu.SemaphoreType.DMA((2, 2)),
            pltpu.SemaphoreType.DMA((stages, count)),
            pltpu.SemaphoreType.DMA((stages, count)),
            pltpu.SemaphoreType.DMA,
            pltpu.SemaphoreType.DMA((groups - 1,)),
            pltpu.SemaphoreType.DMA((groups - 1,)),
        ],
        compiler_params=pltpu.CompilerParams(collective_id=0, has_side_effects=True, vmem_limit_bytes=56 * 2**20),
        cost_estimate=pl.CostEstimate(
            flops=4 * rows * depth * count * block,
            bytes_accessed=4 * depth * count * block,
            transcendentals=4 * rows * count * block,
        ),
    )(inputs, jnp.transpose(gate_weight, (1, 0, 2)), jnp.transpose(up_weight, (1, 0, 2)), table)


def reversed_bits(axis, bits):
    me = lax.axis_index(axis)
    return sum(lax.rem(me // (1 << bit), 2) * (1 << (bits - 1 - bit)) for bit in range(bits))


def down_kernel(levels, folds, span, *refs):
    rotated_ref, down_ref, out_ref, gathered, weights, total = refs[:6]
    rest = list(refs[6:])
    sends, rest = rest[:folds], rest[folds:]
    arrivals, rest = rest[:folds], rest[folds:]
    keeps, rest = rest[:folds], rest[folds:]
    weight_sem, send_sem, recv_sem, fold_send_sem, fold_recv_sem = rest
    own = rotated_ref.shape[0]
    rows, width = total.shape
    chunks = gathered.shape[0]
    groups = 1 << levels
    block = out_ref.shape[0]
    tiles = max(1, min(4, width // 128))
    tile_width = width // tiles
    place = reversed_bits("dp", levels)
    spread = [partner_of("dp", levels - 1 - stage) for stage in range(levels)]
    folded = [partner_of("tensor", level) for level in range(folds)]

    def fetch(chunk):
        source = down_ref.at[pl.ds(pl.multiple_of(chunk * span, span), span), :]
        return pltpu.make_async_copy(source, weights.at[chunk], weight_sem.at[chunk])

    def prefetch(chunk, carry):
        fetch(chunk).start()
        return carry

    lax.fori_loop(0, chunks, prefetch, 0)
    barrier = pltpu.get_barrier_semaphore()
    for partner, _ in spread:
        pl.semaphore_signal(barrier, inc=1, device_id={"dp": partner}, device_id_type=pl.DeviceIdType.MESH)
    for partner, _ in folded:
        pl.semaphore_signal(barrier, inc=1, device_id={"tensor": partner}, device_id_type=pl.DeviceIdType.MESH)
    mine = pl.ds(pl.multiple_of(place * own, own), own)
    for chunk in range(chunks):
        gathered[chunk, mine, :] = rotated_ref[:, chunk * span : (chunk + 1) * span]
    pl.semaphore_wait(barrier, levels + folds)

    def transfer(stage, chunk):
        size = own << stage
        start = place // (1 << stage) * size
        held = gathered.at[chunk, pl.ds(pl.multiple_of(start, size), size), :]
        return pltpu.make_async_remote_copy(
            src_ref=held,
            dst_ref=held,
            send_sem=send_sem.at[stage, chunk],
            recv_sem=recv_sem.at[stage, chunk],
            device_id={"dp": spread[stage][0]},
            device_id_type=pl.DeviceIdType.MESH,
        )

    def relay(stage, chunk):
        if stage > 0:
            transfer(stage - 1, chunk).wait_recv()
        transfer(stage, chunk).start()

    def natural(block_index):
        return sum((block_index >> bit & 1) << (levels - 1 - bit) for bit in range(levels))

    def multiply(chunk):
        transfer(levels - 1, chunk).wait_recv()
        fetch(chunk).wait()
        left = jnp.concatenate(
            [gathered[chunk, natural(p) * own : (natural(p) + 1) * own, :] for p in range(groups)], axis=0
        )
        for tile in range(tiles):
            cols = slice(tile * tile_width, (tile + 1) * tile_width)
            total[:, cols] += jnp.dot(left, weights[chunk, :, cols], preferred_element_type=jnp.float32)

    total[...] = jnp.zeros_like(total)
    steps = [functools.partial(relay, stage) for stage in range(levels)] + [multiply]

    def iteration(turn, carry):
        for order, step in enumerate(steps):
            chunk = turn - order * LAG

            @pl.when((chunk >= 0) & (chunk < chunks))
            def _(step=step, chunk=chunk):
                step(chunk)

        return carry

    lax.fori_loop(0, chunks + (len(steps) - 1) * LAG, iteration, 0)

    def fold(level, tile):
        cols = pl.ds(tile * tile_width, tile_width)
        return pltpu.make_async_remote_copy(
            src_ref=sends[level].at[:, cols],
            dst_ref=arrivals[level].at[:, cols],
            send_sem=fold_send_sem.at[level, tile],
            recv_sem=fold_recv_sem.at[level, tile],
            device_id={"tensor": folded[level][0]},
            device_id_type=pl.DeviceIdType.MESH,
        )

    def part_of(level, index, bit):
        source = total if level == 0 else keeps[level - 1]
        return source, pl.ds(pl.multiple_of((2 * index + bit) * block, block), block)

    def give(level, tile):
        cols = slice(tile * tile_width, (tile + 1) * tile_width)
        for index in range(1 << (folds - 1 - level)):
            source, at = part_of(level, index, 1 - folded[level][1])
            sends[level][index * block : (index + 1) * block, cols] = source[at, cols]
        fold(level, tile).start()

    for tile in range(tiles):
        give(0, tile)
    for level in range(folds):
        for tile in range(tiles):
            cols = slice(tile * tile_width, (tile + 1) * tile_width)
            fold(level, tile).wait_recv()
            target = out_ref if level + 1 == folds else keeps[level]
            for index in range(1 << (folds - 1 - level)):
                source, at = part_of(level, index, folded[level][1])
                span_of = slice(index * block, (index + 1) * block)
                target[span_of, cols] = source[at, cols] + arrivals[level][span_of, cols]
            if level + 1 < folds:
                give(level + 1, tile)

    def drain(chunk, carry):
        for stage in range(levels):
            transfer(stage, chunk).wait_send()
        return carry

    lax.fori_loop(0, chunks, drain, 0)
    for level in range(folds):
        for tile in range(tiles):
            fold(level, tile).wait_send()


def mixed_rows(rotated, down_flat, count, groups, tensor):
    own, hidden = rotated.shape
    width = down_flat.shape[1]
    rows = own * groups
    levels = groups.bit_length() - 1
    folds = tensor.bit_length() - 1
    chunks = count // 2
    span = hidden // chunks
    block = rows // tensor
    tiles = max(1, min(4, width // 128))
    halves = [pltpu.VMEM((rows >> (level + 1), width), jnp.float32) for level in range(folds)]
    vmem = pl.BlockSpec(memory_space=pltpu.VMEM)
    return pl.pallas_call(
        functools.partial(down_kernel, levels, folds, span),
        out_shape=jax.ShapeDtypeStruct((block, width), jnp.float32),
        in_specs=[vmem, pl.BlockSpec(memory_space=pl.ANY)],
        out_specs=vmem,
        scratch_shapes=[
            pltpu.VMEM((chunks, rows, span), jnp.bfloat16),
            pltpu.VMEM((chunks, span, width), jnp.bfloat16),
            pltpu.VMEM((rows, width), jnp.float32),
            *halves,
            *halves,
            *halves,
            pltpu.SemaphoreType.DMA((chunks,)),
            pltpu.SemaphoreType.DMA((levels, chunks)),
            pltpu.SemaphoreType.DMA((levels, chunks)),
            pltpu.SemaphoreType.DMA((folds, tiles)),
            pltpu.SemaphoreType.DMA((folds, tiles)),
        ],
        compiler_params=pltpu.CompilerParams(collective_id=1, has_side_effects=True, vmem_limit_bytes=56 * 2**20),
        cost_estimate=pl.CostEstimate(
            flops=2 * rows * hidden * width, bytes_accessed=2 * hidden * width, transcendentals=0
        ),
    )(rotated, down_flat)


def per_device(groups, tensor, inputs, gate_weight, up_weight, down_weight):
    kernel_a, block_e, width = down_weight.shape
    rotated = rotated_hidden(inputs, gate_weight, up_weight, groups, tensor)
    return mixed_rows(rotated, down_weight.reshape(kernel_a * block_e, width), kernel_a, groups, tensor)


def solution(mesh):
    return jax.shard_map(
        functools.partial(per_device, mesh.shape["dp"], mesh.shape["tensor"]),
        mesh=mesh,
        in_specs=(
            P("dp", None),
            P("dp", None, "tensor"),
            P("dp", None, "tensor"),
            P(None, "tensor", "dp"),
        ),
        out_specs=P("tensor", "dp"),
        check_vma=False,
    )
```
